256 devices in a mesh: energy: 16 (over x, z_lo), tile: 16 (over z_hi, y, core).
Axes of the slice: x: 4, y: 4, z: 8 (z_hi: 2, z_lo: 4; z = z_hi * 4 + z_lo), core: 2. Of those that a mesh axis runs over, the one named last changes fastest.
Arguments:
- object_tiles: float32 [16, 2, 16, 512, 512], P('energy', None, 'tile'), may hold values from -6 to 6
- probe_wave: float32 [16, 2, 256, 256], P('energy'), may hold values from -6 to 6
- measured: bfloat16 [16, 16, 16, 256, 256], P('energy', 'tile'), may hold values from 0 to 2
- positions: int32 [16, 16, 2], P('tile'), may hold values from 0 to 511, as said below
- materials: float32 [2, 16, 8], replicated, may hold values from -6 to 6
Outputs:
- fitted: float32 [16, 2, 16, 512, 512], P('energy', None, 'tile')
The draws below stay inside these ranges and needn't reach their ends.
Inputs may be any that keep to these rules, and one draw needn't show every extreme that they name: `positions`: each entry is the corner of a 256 x 256 patch, given inside its tile; in every tile some patch has row corner 512 - 1 and some has column corner 512 - 1.
All inputs are finite; a program needn't handle non-finite values.
Results may differ from the reference program's by a relative error of at most 0.0013.
Values sent between devices are 32-bit elements; how exact they have to be, the bound alone decides.
No kernel may reach another device: no remote copies, remote signals or barrier semaphores. Data moves between devices by JAX's collectives and lax.ppermute only.
A program may use at most 64 MiB of HBM per device.

```python
import math
import jax
import jax.numpy as jnp
from jax import lax

PATCH = 256
TILE_PX = 512
TILE_COLS = 4
PATCHES = 16
MATERIALS = 8
FIT_STEPS = 10
ENERGIES = 16
TILES = 16


def draw_positions(key, part):
    base = jax.random.fold_in(key, 11)
    row_key, col_key = jax.random.split(base)
    row_draw = jax.random.randint(row_key, (TILES, PATCHES), 0, TILE_PX, dtype=jnp.int32)
    col_draw = jax.random.randint(col_key, (TILES, PATCHES), 0, TILE_PX, dtype=jnp.int32)
    col_draw = col_draw.at[:, 0].set(TILE_PX - 1)
    row_draw = row_draw.at[:, 1].set(TILE_PX - 1)
    col_draw = col_draw.at[:, 1].set(TILE_PX - 1)
    corners = jnp.stack([row_draw, col_draw], -1).astype(jnp.int32)
    return corners


def steps_of(key, shape, cuts, smallest, top_value):
    def one(position, blocks):
        steps = jax.random.uniform(jax.random.fold_in(jax.random.fold_in(key, 6), position), (blocks,), jnp.float32, smallest / len(cuts), top_value / len(cuts))
        return jnp.repeat(jnp.exp(steps), shape[position] // blocks).reshape((-1,) + (1,) * (len(shape) - position - 1))

    gain = one(*cuts[0])
    for cut in cuts[1:]:
        gain = gain * one(*cut)
    return gain


def normal_values(stream_key, extent, width, limit, pieces=(), kind=jnp.bfloat16):
    level = steps_of(stream_key, extent, pieces, -0.22, 0.18) if pieces else 1.0
    entries = jax.random.normal(stream_key, extent, jnp.float32) * width * level
    return jnp.minimum(jnp.maximum(entries, -limit), limit).astype(kind)


def setup_inputs(seed: int = 0) -> dict:
    key_list = jax.random.split(jax.random.key(seed), 6)
    object_tiles = normal_values(key_list[0], (ENERGIES, 2, TILES, TILE_PX, TILE_PX), 1.0, 6.0, ((0, 16), (2, 16)), jnp.float32)
    probe_wave = normal_values(key_list[1], (ENERGIES, 2, PATCH, PATCH), 1.0, 6.0, ((0, 16),), jnp.float32)
    measured = jnp.clip(2.0 * jax.random.uniform(key_list[2], (ENERGIES, TILES, PATCHES, PATCH, PATCH), jnp.float32) ** steps_of(key_list[2], (ENERGIES, TILES, PATCHES, PATCH, PATCH), ((0, 16), (1, 16)), -0.2, 0.2), 0.0, 2.0).astype(jnp.bfloat16)
    positions = draw_positions(jax.random.fold_in(key_list[5], 71), 0)
    materials = normal_values(key_list[4], (2, ENERGIES, MATERIALS), 1.0, 6.0, (), jnp.float32)
    return {"object_tiles": object_tiles, "probe_wave": probe_wave, "measured": measured, "positions": positions, "materials": materials}


amplitude_floor = 0.5

def fourier_tables(length, direction):
    counter = jnp.arange(length, dtype=jnp.int32)
    products = counter[:, None] * counter[None, :] % length
    angles = 2.0 * math.pi / length * products.astype(jnp.float32)
    cosine = jnp.cos(angles)
    sine = direction * jnp.sin(angles)
    left_table = jnp.concatenate([jnp.concatenate([cosine, sine], 1), jnp.concatenate([-sine, cosine], 1)], 0).astype(jnp.bfloat16)
    right_table = jnp.concatenate([jnp.concatenate([cosine, -sine], 1), jnp.concatenate([sine, cosine], 1)], 0).astype(jnp.bfloat16)
    return (left_table, right_table)

def transform(real_part, imag_part, left_table, right_table):
    length = real_part.shape[0]
    stacked = jnp.concatenate([real_part, imag_part], 0).astype(jnp.bfloat16)
    inner = jnp.dot(left_table, stacked, preferred_element_type=jnp.float32)
    beside = jnp.concatenate([inner[:length], inner[length:]], 1).astype(jnp.bfloat16)
    outer = jnp.dot(beside, right_table, preferred_element_type=jnp.float32) / length
    return (outer[:, :length], outer[:, length:])

def patch_gradient(field_real, field_imag, probe_real, probe_imag, amplitude, row_start, col_start, tables):
    length = probe_real.shape[0]
    piece_real = lax.dynamic_slice(field_real, (row_start, col_start), (length, length))
    piece_imag = lax.dynamic_slice(field_imag, (row_start, col_start), (length, length))
    exit_real = probe_real * piece_real - probe_imag * piece_imag
    exit_imag = probe_real * piece_imag + probe_imag * piece_real
    far_real, far_imag = transform(exit_real, exit_imag, tables[0], tables[1])
    magnitude = jnp.sqrt(far_real * far_real + far_imag * far_imag)
    factor = amplitude.astype(jnp.float32) / jnp.maximum(magnitude, amplitude_floor) - 1.0
    back_real, back_imag = transform(factor * far_real, factor * far_imag, tables[2], tables[3])
    return (probe_real * back_real + probe_imag * back_imag, probe_real * back_imag - probe_imag * back_real)

def fit_materials(data, materials):
    high = lax.Precision.HIGHEST
    gram = jnp.einsum('rem,ren->mn', materials, materials, precision=high)
    rate = 1.0 / jnp.trace(gram)
    target = jnp.einsum('rem,rep->mp', materials, data, precision=high)

    def descend(number, coefficients):
        slope = jnp.dot(gram, coefficients, precision=high) - target
        return jnp.maximum(coefficients - rate * slope, 0.0)
    return lax.fori_loop(0, FIT_STEPS, descend, jnp.zeros_like(target))

def energy_update(object_one, probe_one, measured_one, positions):
    right_strip = jnp.roll(object_one, -1, axis=1)[:, :, :, :PATCH]
    widened = jnp.concatenate([object_one, right_strip], 3)
    lower_strip = jnp.roll(widened, -TILE_COLS, axis=1)[:, :, :PATCH, :]
    extended = jnp.concatenate([widened, lower_strip], 2)
    forward = fourier_tables(PATCH, 1.0)
    inverse = fourier_tables(PATCH, -1.0)
    tables = (forward[0], forward[1], inverse[0], inverse[1])
    flat_measured = measured_one.reshape(TILES * PATCHES, PATCH, PATCH)
    flat_corners = positions.reshape(TILES * PATCHES, 2)
    anchor = jnp.zeros((), jnp.int32)

    def accumulate(number, gradient):
        tile_index = (number // PATCHES).astype(jnp.int32)
        row_start = flat_corners[number, 0].astype(jnp.int32)
        col_start = flat_corners[number, 1].astype(jnp.int32)
        field = lax.dynamic_index_in_dim(extended, tile_index, 1, False)
        term_real, term_imag = patch_gradient(field[0], field[1], probe_one[0], probe_one[1], flat_measured[number], row_start, col_start, tables)
        current = lax.dynamic_slice(gradient, (anchor, tile_index, row_start, col_start), (2, 1, PATCH, PATCH))
        added = current + jnp.stack([term_real, term_imag])[:, None]
        return lax.dynamic_update_slice(gradient, added, (anchor, tile_index, row_start, col_start))
    gradient = lax.fori_loop(0, TILES * PATCHES, accumulate, jnp.zeros_like(extended))
    from_above = jnp.roll(gradient[:, :, TILE_PX:, :], TILE_COLS, axis=1)
    upper = jnp.concatenate([gradient[:, :, :PATCH, :] + from_above, gradient[:, :, PATCH:TILE_PX, :]], 2)
    from_left = jnp.roll(upper[:, :, :, TILE_PX:], 1, axis=1)
    summed = jnp.concatenate([upper[:, :, :, :PATCH] + from_left, upper[:, :, :, PATCH:TILE_PX]], 3)
    peak = jnp.max(probe_one[0] * probe_one[0] + probe_one[1] * probe_one[1])
    return object_one + summed / peak

def reference(object_tiles, probe_wave, measured, positions, materials):
    updated = lax.map(lambda inputs: energy_update(inputs[0], inputs[1], inputs[2], positions), (object_tiles, probe_wave, measured))
    data = updated.transpose(1, 0, 2, 3, 4).reshape(2, ENERGIES, TILES * TILE_PX * TILE_PX)
    coefficients = fit_materials(data, materials)
    spectra = jnp.einsum('rem,mp->rep', materials, coefficients, precision=lax.Precision.HIGHEST)
    spectra = spectra.reshape(2, ENERGIES, TILES, TILE_PX, TILE_PX).transpose(1, 0, 2, 3, 4)
    return spectra
```

```python
import functools

import jax
import jax.numpy as jnp
import ml_dtypes
import numpy as np
from jax import lax
from jax.experimental import pallas as pl
from jax.experimental.pallas import tpu as pltpu
from jax.sharding import PartitionSpec as P

TILE_COLS = 4
FIT_STEPS = 10
AMPLITUDE_FLOOR = 0.5
LANES = 128
VMEM_BYTES = 48 * 2**20


def shifted(value, axis, steps):
    count = lax.axis_size(axis)
    pairs = [(source, (source + steps) % count) for source in range(count)]
    return lax.ppermute(value, axis, pairs)


def fourier_tables(length):
    counter = np.arange(length)
    angles = 2.0 * np.pi / length * (counter[:, None] * counter[None, :] % length)
    cosine, sine = np.cos(angles), np.sin(angles)
    left_table = np.block([[cosine, sine], [-sine, cosine]])
    right_table = np.block([[cosine, -sine], [sine, cosine]])
    return [t.astype(np.float32).astype(ml_dtypes.bfloat16) for t in (left_table, right_table)]


def transform(real_part, imag_part, left_table, right_table):
    length = real_part.shape[0]
    stacked = jnp.concatenate([real_part, imag_part], 0).astype(jnp.bfloat16)
    inner = jnp.dot(left_table, stacked, preferred_element_type=jnp.float32).astype(jnp.bfloat16)
    beside = jnp.concatenate([inner[:length], inner[length:]], 1)
    outer = jnp.dot(beside, right_table, preferred_element_type=jnp.float32)
    return outer[:, :length], outer[:, length:]


def gradient_kernel(
    corners, own, right, lower, corner, probe, measured, left_table, right_table,
    main_out, right_out, lower_out, corner_out, field, grad,
):
    count, length = measured.shape[0], measured.shape[1]
    tile_px = own.shape[1]
    across, beyond = tile_px // LANES, length // LANES
    for part in range(2):
        for block in range(across):
            cols = slice(block * LANES, (block + 1) * LANES)
            field[part, block, :tile_px, :] = own[part, :, cols]
            field[part, block, tile_px:, :] = lower[part, :, cols]
        for block in range(beyond):
            cols = slice(block * LANES, (block + 1) * LANES)
            field[part, across + block, :tile_px, :] = right[part, :, cols]
            field[part, across + block, tile_px:, :] = corner[part, :, cols]
    grad[...] = jnp.zeros_like(grad)
    lane = lax.broadcasted_iota(jnp.int32, (length, LANES), 1)
    floor = (AMPLITUDE_FLOOR * length) ** 2

    def add_patch(number, carry):
        row, col = corners[number, 0], corners[number, 1]
        block, shift = col // LANES, col % LANES
        rows = pl.ds(row, length)
        head = lane < LANES - shift
        piece = []
        for part in range(2):
            turned = [
                pltpu.roll(field[part, block + i, rows, :], (LANES - shift) % LANES, 1)
                for i in range(beyond + 1)
            ]
            piece.append(
                jnp.concatenate(
                    [jnp.where(head, turned[i], turned[i + 1]) for i in range(beyond)], 1
                )
            )
        probe_real, probe_imag = probe[0], probe[1]
        exit_real = probe_real * piece[0] - probe_imag * piece[1]
        exit_imag = probe_real * piece[1] + probe_imag * piece[0]
        far_real, far_imag = transform(exit_real, exit_imag, left_table[...], right_table[...])
        power = jnp.maximum(far_real * far_real + far_imag * far_imag, floor)
        factor = measured[number].astype(jnp.float32) * (length * lax.rsqrt(power)) - 1.0
        back_real, back_imag = transform(
            factor * far_real, factor * far_imag, right_table[...], left_table[...]
        )
        terms = (
            probe_real * back_real + probe_imag * back_imag,
            probe_real * back_imag - probe_imag * back_real,
        )
        tail = lane >= shift
        for part in range(2):
            turned = [
                pltpu.roll(terms[part][:, i * LANES : (i + 1) * LANES], shift, 1)
                for i in range(beyond)
            ]
            grad[part, block, rows, :] += jnp.where(tail, turned[0], 0.0)
            for i in range(1, beyond):
                grad[part, block + i, rows, :] += jnp.where(tail, turned[i], turned[i - 1])
            grad[part, block + beyond, rows, :] += jnp.where(tail, 0.0, turned[beyond - 1])
        return carry

    lax.fori_loop(0, count, add_patch, 0)
    peak = jnp.max(probe[0] * probe[0] + probe[1] * probe[1], keepdims=True)
    scale = 1.0 / (peak * float(length * length))
    for part in range(2):
        for block in range(across):
            cols = slice(block * LANES, (block + 1) * LANES)
            main_out[part, :, cols] = own[part, :, cols] + grad[part, block, :tile_px, :] * scale
            lower_out[part, :, cols] = grad[part, block, tile_px:, :] * scale
        for block in range(beyond):
            cols = slice(block * LANES, (block + 1) * LANES)
            right_out[part, :, cols] = grad[part, across + block, :tile_px, :] * scale
            corner_out[part, :, cols] = grad[part, across + block, tile_px:, :] * scale


def patch_gradients(corners, own, right, lower, corner, probe, measured):
    count, length = measured.shape[0], measured.shape[1]
    tile_px = own.shape[1]
    left_table, right_table = (jnp.asarray(t) for t in fourier_tables(length))
    extent = tile_px + length
    vmem = pl.BlockSpec(memory_space=pltpu.VMEM)
    plane = pltpu.VMEM((2, extent // LANES, extent, LANES), jnp.float32)
    f32 = functools.partial(jax.ShapeDtypeStruct, dtype=jnp.float32)
    return pl.pallas_call(
        gradient_kernel,
        out_shape=[
            f32((2, tile_px, tile_px)),
            f32((2, tile_px, length)),
            f32((2, length, tile_px)),
            f32((2, length, length)),
        ],
        in_specs=[pl.BlockSpec(memory_space=pltpu.SMEM)] + [vmem] * 8,
        out_specs=[vmem] * 4,
        scratch_shapes=[plane, plane],
        compiler_params=pltpu.CompilerParams(vmem_limit_bytes=VMEM_BYTES),
        cost_estimate=pl.CostEstimate(
            flops=count * 32 * length**3, bytes_accessed=2**23, transcendentals=0
        ),
        name="patch_gradients",
    )(corners, own, right, lower, corner, probe, measured, left_table, right_table)


def fit_kernel(spectra, step, rate, data, fitted):
    energies, _, rows, width = data.shape
    materials = step.shape[0]
    cols = 2 * LANES
    blocks = width // cols

    def fit_block(number, carry):
        row = pl.multiple_of(number // blocks * 8, 8)
        col = pl.multiple_of(number % blocks * cols, cols)
        here = (pl.ds(row, 8), pl.ds(col, cols))
        target = [None] * materials
        for part in range(2):
            for energy in range(energies):
                value = data[(energy, part) + here]
                for m in range(materials):
                    term = spectra[part, energy * materials + m] * value
                    target[m] = term if target[m] is None else target[m] + term
        target = [rate[0] * value for value in target]
        start = tuple(jnp.maximum(value, 0.0) for value in target)

        def descend(number, coefficients):
            moved = []
            for m in range(materials):
                total = target[m]
                for n in range(materials):
                    total = total + step[m, n] * coefficients[n]
                moved.append(jnp.maximum(total, 0.0))
            return tuple(moved)

        coefficients = lax.fori_loop(1, FIT_STEPS, descend, start)
        for part in range(2):
            for energy in range(energies):
                total = spectra[part, energy * materials] * coefficients[0]
                for m in range(1, materials):
                    total = total + spectra[part, energy * materials + m] * coefficients[m]
                fitted[(energy, part) + here] = total
        return carry

    lax.fori_loop(0, rows // 8 * blocks, fit_block, 0)


def fit_spectra(data, materials):
    gram = jnp.einsum("rem,ren->mn", materials, materials, precision=lax.Precision.HIGHEST)
    rate = 1.0 / jnp.trace(gram)
    step = jnp.eye(gram.shape[0], dtype=jnp.float32) - rate * gram
    smem = pl.BlockSpec(memory_space=pltpu.SMEM)
    vmem = pl.BlockSpec(memory_space=pltpu.VMEM)
    return pl.pallas_call(
        fit_kernel,
        out_shape=jax.ShapeDtypeStruct(data.shape, jnp.float32),
        in_specs=[smem, smem, smem, vmem],
        out_specs=vmem,
        compiler_params=pltpu.CompilerParams(vmem_limit_bytes=VMEM_BYTES),
        name="fit_spectra",
    )(materials.reshape(2, -1), step, rate.reshape(1), data)


def body(object_tiles, probe_wave, measured, positions, materials):
    own = object_tiles[0, :, 0]
    tile_px = own.shape[-1]
    length = probe_wave.shape[-1]
    row_step = TILE_COLS % lax.axis_size("tile")
    right = shifted(own[:, :, :length], "tile", -1)
    lower = shifted(own[:, :length, :], "tile", -row_step)
    corner = shifted(lower[:, :, :length], "tile", -1)
    main, to_right, to_lower, to_corner = patch_gradients(
        positions[0], own, right, lower, corner, probe_wave[0], measured[0, 0]
    )
    from_left = shifted(to_right, "tile", 1)
    beside = shifted(to_corner, "tile", 1)
    lowered = jnp.concatenate([to_lower[:, :, :length] + beside, to_lower[:, :, length:]], 2)
    from_above = shifted(lowered, "tile", row_step)
    updated = (
        main
        + jnp.pad(from_left, ((0, 0), (0, 0), (0, tile_px - length)))
        + jnp.pad(from_above, ((0, 0), (0, tile_px - length), (0, 0)))
    )
    groups = lax.axis_size("energy")
    outgoing = updated.reshape(2, groups, tile_px // groups, tile_px).transpose(1, 0, 2, 3)
    arrived = lax.all_to_all(outgoing, "energy", split_axis=0, concat_axis=0, tiled=True)
    spectra = fit_spectra(arrived, materials)
    returned = lax.all_to_all(spectra, "energy", split_axis=0, concat_axis=0, tiled=True)
    return returned.transpose(1, 0, 2, 3).reshape(1, 2, 1, tile_px, tile_px)


def solution(mesh):
    in_specs = (
        P("energy", None, "tile", None, None),
        P("energy", None, None, None),
        P("energy", "tile", None, None, None),
        P("tile", None, None),
        P(),
    )
    out_specs = P("energy", None, "tile", None, None)
    return jax.shard_map(body, mesh=mesh, in_specs=in_specs, out_specs=out_specs, check_vma=False)
```

```python
import functools
import math

import jax
import jax.numpy as jnp
import ml_dtypes
import numpy as np
from jax import lax
from jax.experimental import pallas as pl
from jax.experimental.pallas import tpu as pltpu
from jax.sharding import PartitionSpec as P

TILE_COLS = 4
FIT_STEPS = 10
AMPLITUDE_FLOOR = 0.5
LANES = 128
GROUP = 4
VMEM_BYTES = 48 * 2**20


def fourier_tables(length):
    counter = np.arange(length)
    angles = 2.0 * np.pi / length * (counter[:, None] * counter[None, :] % length)
    cosine, sine = np.cos(angles), np.sin(angles)
    left_table = np.block([[cosine, sine], [-sine, cosine]])
    right_table = np.block([[cosine, -sine], [sine, cosine]])
    return [t.astype(np.float32).astype(ml_dtypes.bfloat16) for t in (left_table, right_table)]


def times(left, right):
    return jnp.dot(left, right, preferred_element_type=jnp.float32)


def transforms(stacked, left_table, right_table):
    length = stacked[0].shape[1]
    inner = [times(left_table, value).astype(jnp.bfloat16) for value in stacked]
    beside = [jnp.concatenate([value[:length], value[length:]], 1) for value in inner]
    return [times(value, right_table) for value in beside]


def stack(real_part, imag_part):
    return jnp.concatenate([real_part.astype(jnp.bfloat16), imag_part.astype(jnp.bfloat16)], 0)


def gradient_kernel(
    corners, own, right, right_far, lower_left, lower_right, corner, corner_far, probe, measured,
    left_table, right_table, main_out, right_out, lower_left_out, lower_right_out, corner_out,
    field, grad,
):
    count, length = measured.shape[0], measured.shape[1]
    tile_px = own.shape[1]
    across, beyond = tile_px // LANES, length // LANES
    for part in range(2):
        for block in range(across):
            cols = slice(block * LANES, (block + 1) * LANES)
            field[part, block, :tile_px, :] = own[part, :, cols]
        for block in range(beyond):
            cols = slice(block * LANES, (block + 1) * LANES)
            field[part, block, tile_px:, :] = lower_left[part, :, cols]
            field[part, beyond + block, tile_px:, :] = lower_right[part, :, cols]
            field[part, across + block, :tile_px, :] = right[part, :, cols] + right_far[part, :, cols]
            field[part, across + block, tile_px:, :] = (
                corner[part, :, cols] + corner_far[part, :, cols]
            )
    grad[...] = jnp.zeros_like(grad)
    lane = lax.broadcasted_iota(jnp.int32, (length, LANES), 1)
    floor = (AMPLITUDE_FLOOR * length) ** 2

    def place(number):
        row, col = corners[number, 0], corners[number, 1]
        return pl.ds(row, length), col // LANES, col % LANES

    def exit_wave(number):
        rows, block, shift = place(number)
        head = lane < LANES - shift
        piece = []
        for part in range(2):
            turned = [
                pltpu.roll(field[part, block + i, rows, :], (LANES - shift) % LANES, 1)
                for i in range(beyond + 1)
            ]
            piece.append(
                jnp.concatenate(
                    [jnp.where(head, turned[i], turned[i + 1]) for i in range(beyond)], 1
                )
            )
        probe_real, probe_imag = probe[0], probe[1]
        return stack(
            probe_real * piece[0] - probe_imag * piece[1],
            probe_real * piece[1] + probe_imag * piece[0],
        )

    def change(number, far):
        far_real, far_imag = far[:, :length], far[:, length:]
        power = jnp.maximum(far_real * far_real + far_imag * far_imag, floor)
        factor = measured[number].astype(jnp.float32) * (length * lax.rsqrt(power)) - 1.0
        return stack(factor * far_real, factor * far_imag)

    def add_terms(number, back):
        rows, block, shift = place(number)
        probe_real, probe_imag = probe[0], probe[1]
        back_real, back_imag = back[:, :length], back[:, length:]
        terms = (
            probe_real * back_real + probe_imag * back_imag,
            probe_real * back_imag - probe_imag * back_real,
        )
        tail = lane >= shift
        for part in range(2):
            turned = [
                pltpu.roll(terms[part][:, i * LANES : (i + 1) * LANES], shift, 1)
                for i in range(beyond)
            ]
            grad[part, block, rows, :] += jnp.where(tail, turned[0], 0.0)
            for i in range(1, beyond):
                grad[part, block + i, rows, :] += jnp.where(tail, turned[i], turned[i - 1])
            grad[part, block + beyond, rows, :] += jnp.where(tail, 0.0, turned[beyond - 1])

    group = math.gcd(GROUP, count)

    def add_group(first, carry):
        numbers = [first * group + i for i in range(group)]
        waves = [exit_wave(number) for number in numbers]
        far = transforms(waves, left_table[...], right_table[...])
        changes = [change(number, value) for number, value in zip(numbers, far)]
        back = transforms(changes, right_table[...], left_table[...])
        for number, value in zip(numbers, back):
            add_terms(number, value)
        return carry

    lax.fori_loop(0, count // group, add_group, 0)
    peak = jnp.max(probe[0] * probe[0] + probe[1] * probe[1], keepdims=True)
    scale = 1.0 / (peak * float(length * length))
    for part in range(2):
        for block in range(across):
            cols = slice(block * LANES, (block + 1) * LANES)
            main_out[part, :, cols] = own[part, :, cols] + grad[part, block, :tile_px, :] * scale
        for block in range(beyond):
            cols = slice(block * LANES, (block + 1) * LANES)
            lower_left_out[part, :, cols] = grad[part, block, tile_px:, :] * scale
            lower_right_out[part, :, cols] = grad[part, beyond + block, tile_px:, :] * scale
            right_out[part, :, cols] = grad[part, across + block, :tile_px, :] * scale
            corner_out[part, :, cols] = grad[part, across + block, tile_px:, :] * scale


def patch_gradients(corners, own, halos, probe, measured):
    count, length = measured.shape[0], measured.shape[1]
    tile_px = own.shape[1]
    left_table, right_table = (jnp.asarray(t) for t in fourier_tables(length))
    extent = tile_px + length
    vmem = pl.BlockSpec(memory_space=pltpu.VMEM)
    plane = pltpu.VMEM((2, extent // LANES, extent, LANES), jnp.float32)
    f32 = functools.partial(jax.ShapeDtypeStruct, dtype=jnp.float32)
    square = f32((2, length, length))
    return pl.pallas_call(
        gradient_kernel,
        out_shape=[
            f32((2, tile_px, tile_px)), f32((2, tile_px, length)), square, square, square,
        ],
        in_specs=[pl.BlockSpec(memory_space=pltpu.SMEM)] + [vmem] * 11,
        out_specs=[vmem] * 5,
        scratch_shapes=[plane, plane],
        compiler_params=pltpu.CompilerParams(vmem_limit_bytes=VMEM_BYTES),
        cost_estimate=pl.CostEstimate(
            flops=count * 32 * length**3, bytes_accessed=2**23, transcendentals=0
        ),
        name="patch_gradients",
    )(corners, own, *halos, probe, measured, left_table, right_table)


def fit_kernel(spectra, step, rate, data, fitted):
    energies, _, rows, width = data.shape
    materials = step.shape[0]
    cols = 2 * LANES
    blocks = width // cols

    def fit_block(number, carry):
        row = pl.multiple_of(number // blocks * 8, 8)
        col = pl.multiple_of(number % blocks * cols, cols)
        here = (pl.ds(row, 8), pl.ds(col, cols))
        target = [None] * materials
        for part in range(2):
            for energy in range(energies):
                value = data[(energy, part) + here]
                for m in range(materials):
                    term = spectra[part, energy * materials + m] * value
                    target[m] = term if target[m] is None else target[m] + term
        target = [rate[0] * value for value in target]
        start = tuple(jnp.maximum(value, 0.0) for value in target)

        def descend(number, coefficients):
            moved = []
            for m in range(materials):
                total = target[m]
                for n in range(materials):
                    total = total + step[m, n] * coefficients[n]
                moved.append(jnp.maximum(total, 0.0))
            return tuple(moved)

        coefficients = lax.fori_loop(1, FIT_STEPS, descend, start)
        for part in range(2):
            for energy in range(energies):
                total = spectra[part, energy * materials] * coefficients[0]
                for m in range(1, materials):
                    total = total + spectra[part, energy * materials + m] * coefficients[m]
                fitted[(energy, part) + here] = total
        return carry

    lax.fori_loop(0, rows // 8 * blocks, fit_block, 0)


def fit_spectra(data, materials):
    gram = jnp.einsum("rem,ren->mn", materials, materials, precision=lax.Precision.HIGHEST)
    rate = 1.0 / jnp.trace(gram)
    step = jnp.eye(gram.shape[0], dtype=jnp.float32) - rate * gram
    smem = pl.BlockSpec(memory_space=pltpu.SMEM)
    vmem = pl.BlockSpec(memory_space=pltpu.VMEM)
    return pl.pallas_call(
        fit_kernel,
        out_shape=jax.ShapeDtypeStruct(data.shape, jnp.float32),
        in_specs=[smem, smem, smem, vmem],
        out_specs=vmem,
        compiler_params=pltpu.CompilerParams(vmem_limit_bytes=VMEM_BYTES),
        name="fit_spectra",
    )(materials.reshape(2, -1), step, rate.reshape(1), data)


def body(object_tiles, probe_wave, measured, positions, materials):
    own = object_tiles[0, :, 0]
    tile_px = own.shape[-1]
    length = probe_wave.shape[-1]
    tiles = lax.axis_size("tile")
    half = tiles // 2
    last = half - 1

    def move(value, pairs):
        return lax.ppermute(value, "tile", [(s % tiles, d % tiles) for s, d in pairs])

    lower_left = move(own[:, :length, :length], [(t, t - TILE_COLS) for t in range(tiles)])
    right_step = move(own[:, :, :length], [(0, last), (half, half + last)])
    corner_step = move(
        own[:, :length, :length], [(TILE_COLS, half + TILE_COLS), (half + TILE_COLS, TILE_COLS)]
    )
    right = move(own[:, :, :length], [(t, t - 1) for t in range(tiles) if t % half])
    lower_right = move(own[:, :length, length:], [(t, t - TILE_COLS) for t in range(tiles)])
    right_far = move(right_step, [(last, half + last), (half + last, last)])
    corner_far = move(corner_step, [(TILE_COLS, last), (half + TILE_COLS, half + last)])
    corner = move(lower_left, [(t, t - 1) for t in range(tiles) if t % half])

    halos = (right, right_far, lower_left, lower_right, corner, corner_far)
    main, to_right, to_lower_left, to_lower_right, to_corner = patch_gradients(
        positions[0], own, halos, probe_wave[0], measured[0, 0]
    )
    beside = move(to_corner, [(t, t + 1) for t in range(tiles)])
    above_right = move(to_lower_right, [(t, t + TILE_COLS) for t in range(tiles)])
    left_step = move(to_right, [(last, 0), (half + last, half)])
    left = move(to_right, [(t, t + 1) for t in range(tiles) if t % half != last])
    left_far = move(left_step, [(0, half), (half, 0)])
    above_left = move(to_lower_left + beside, [(t, t + TILE_COLS) for t in range(tiles)])
    above = jnp.concatenate([above_left, above_right], 2)
    updated = (
        main
        + jnp.pad(left + left_far, ((0, 0), (0, 0), (0, tile_px - length)))
        + jnp.pad(above, ((0, 0), (0, tile_px - length), (0, 0)))
    )
    groups = lax.axis_size("energy")
    outgoing = updated.reshape(2, groups, tile_px // groups, tile_px).transpose(1, 0, 2, 3)
    arrived = lax.all_to_all(outgoing, "energy", split_axis=0, concat_axis=0, tiled=True)
    spectra = fit_spectra(arrived, materials)
    returned = lax.all_to_all(spectra, "energy", split_axis=0, concat_axis=0, tiled=True)
    return returned.transpose(1, 0, 2, 3).reshape(1, 2, 1, tile_px, tile_px)


def solution(mesh):
    in_specs = (
        P("energy", None, "tile", None, None),
        P("energy", None, None, None),
        P("energy", "tile", None, None, None),
        P("tile", None, None),
        P(),
    )
    out_specs = P("energy", None, "tile", None, None)
    return jax.shard_map(body, mesh=mesh, in_specs=in_specs, out_specs=out_specs, check_vma=False)
```

```python
import functools
import math

import jax
import jax.numpy as jnp
import ml_dtypes
import numpy as np
from jax import lax
from jax.experimental import pallas as pl
from jax.experimental.pallas import tpu as pltpu
from jax.sharding import PartitionSpec as P

TILE_COLS = 4
FIT_STEPS = 10
AMPLITUDE_FLOOR = 0.5
LANES = 128
GROUP = 8
VMEM_BYTES = 36 * 2**20
SMALL_VMEM_BYTES = 16 * 2**20


def fourier_tables(length):
    counter = np.arange(length)
    angles = 2.0 * np.pi / length * (counter[:, None] * counter[None, :] % length)
    cosine, sine = np.cos(angles), np.sin(angles)
    left_table = np.block([[cosine, sine], [-sine, cosine]])
    right_table = np.block([[cosine, -sine], [sine, cosine]])
    return [t.astype(np.float32).astype(ml_dtypes.bfloat16) for t in (left_table, right_table)]


def times(left, right):
    return jnp.dot(left, right, preferred_element_type=jnp.float32)


def transforms(stacked, left_table, right_table):
    length = stacked[0].shape[1]
    inner = [times(left_table, value).astype(jnp.bfloat16) for value in stacked]
    beside = [jnp.concatenate([value[:length], value[length:]], 1) for value in inner]
    return [times(value, right_table) for value in beside]


def stack(real_part, imag_part):
    return jnp.concatenate([real_part.astype(jnp.bfloat16), imag_part.astype(jnp.bfloat16)], 0)


def gradient_kernel(
    corners, own, right, right_far, lower_left, lower_right, corner, corner_far, probe, measured,
    left_table, right_table, main_out, right_out, lower_left_out, lower_right_out, corner_out,
    field, grad,
):
    count, length = measured.shape[0], measured.shape[1]
    tile_px = own.shape[1]
    across, beyond = tile_px // LANES, length // LANES
    for part in range(2):
        for block in range(across):
            cols = slice(block * LANES, (block + 1) * LANES)
            field[part, block, :tile_px, :] = own[part, :, cols]
        for block in range(beyond):
            cols = slice(block * LANES, (block + 1) * LANES)
            field[part, block, tile_px:, :] = lower_left[part, :, cols]
            field[part, beyond + block, tile_px:, :] = lower_right[part, :, cols]
            field[part, across + block, :tile_px, :] = right[part, :, cols] + right_far[part, :, cols]
            field[part, across + block, tile_px:, :] = (
                corner[part, :, cols] + corner_far[part, :, cols]
            )
    grad[...] = jnp.zeros_like(grad)
    lane = lax.broadcasted_iota(jnp.int32, (length, LANES), 1)
    floor = (AMPLITUDE_FLOOR * length) ** 2

    def place(number):
        row, col = corners[number, 0], corners[number, 1]
        return pl.ds(row, length), col // LANES, col % LANES

    def exit_wave(number):
        rows, block, shift = place(number)
        head = lane < LANES - shift
        piece = []
        for part in range(2):
            turned = [
                pltpu.roll(field[part, block + i, rows, :], (LANES - shift) % LANES, 1)
                for i in range(beyond + 1)
            ]
            piece.append(
                jnp.concatenate(
                    [jnp.where(head, turned[i], turned[i + 1]) for i in range(beyond)], 1
                )
            )
        probe_real, probe_imag = probe[0], probe[1]
        return stack(
            probe_real * piece[0] - probe_imag * piece[1],
            probe_real * piece[1] + probe_imag * piece[0],
        )

    def change(number, far):
        far_real, far_imag = far[:, :length], far[:, length:]
        power = jnp.maximum(far_real * far_real + far_imag * far_imag, floor)
        factor = measured[number].astype(jnp.float32) * (length * lax.rsqrt(power)) - 1.0
        return stack(factor * far_real, factor * far_imag)

    def add_terms(number, back):
        rows, block, shift = place(number)
        probe_real, probe_imag = probe[0], probe[1]
        back_real, back_imag = back[:, :length], back[:, length:]
        terms = (
            probe_real * back_real + probe_imag * back_imag,
            probe_real * back_imag - probe_imag * back_real,
        )
        tail = lane >= shift
        for part in range(2):
            turned = [
                pltpu.roll(terms[part][:, i * LANES : (i + 1) * LANES], shift, 1)
                for i in range(beyond)
            ]
            grad[part, block, rows, :] += jnp.where(tail, turned[0], 0.0)
            for i in range(1, beyond):
                grad[part, block + i, rows, :] += jnp.where(tail, turned[i], turned[i - 1])
            grad[part, block + beyond, rows, :] += jnp.where(tail, 0.0, turned[beyond - 1])

    group = math.gcd(GROUP, count)

    def add_group(first, carry):
        numbers = [first * group + i for i in range(group)]
        waves = [exit_wave(number) for number in numbers]
        far = transforms(waves, left_table[...], right_table[...])
        changes = [change(number, value) for number, value in zip(numbers, far)]
        back = transforms(changes, right_table[...], left_table[...])
        for number, value in zip(numbers, back):
            add_terms(number, value)
        return carry

    lax.fori_loop(0, count // group, add_group, 0)
    peak = jnp.max(probe[0] * probe[0] + probe[1] * probe[1], keepdims=True)
    scale = 1.0 / (peak * float(length * length))
    for part in range(2):
        for block in range(across):
            cols = slice(block * LANES, (block + 1) * LANES)
            main_out[part, :, cols] = own[part, :, cols] + grad[part, block, :tile_px, :] * scale
        for block in range(beyond):
            cols = slice(block * LANES, (block + 1) * LANES)
            lower_left_out[part, :, cols] = grad[part, block, tile_px:, :] * scale
            lower_right_out[part, :, cols] = grad[part, beyond + block, tile_px:, :] * scale
            right_out[part, :, cols] = grad[part, across + block, :tile_px, :] * scale
            corner_out[part, :, cols] = grad[part, across + block, tile_px:, :] * scale


def patch_gradients(corners, own, halos, probe, measured):
    count, length = measured.shape[0], measured.shape[1]
    tile_px = own.shape[1]
    left_table, right_table = (jnp.asarray(t) for t in fourier_tables(length))
    extent = tile_px + length
    vmem = pl.BlockSpec(memory_space=pltpu.VMEM)
    plane = pltpu.VMEM((2, extent // LANES, extent, LANES), jnp.float32)
    f32 = functools.partial(jax.ShapeDtypeStruct, dtype=jnp.float32)
    square = f32((2, length, length))
    return pl.pallas_call(
        gradient_kernel,
        out_shape=[
            f32((2, tile_px, tile_px)), f32((2, tile_px, length)), square, square, square,
        ],
        in_specs=[pl.BlockSpec(memory_space=pltpu.SMEM)] + [vmem] * 11,
        out_specs=[vmem] * 5,
        scratch_shapes=[plane, plane],
        compiler_params=pltpu.CompilerParams(vmem_limit_bytes=VMEM_BYTES),
        cost_estimate=pl.CostEstimate(
            flops=count * 32 * length**3, bytes_accessed=2**23, transcendentals=0
        ),
        name="patch_gradients",
    )(corners, own, *halos, probe, measured, left_table, right_table)


def combine_kernel(main, left, left_far, above_left, above_right, outgoing):
    groups, _, rows, _ = outgoing.shape
    length = left.shape[2]
    for group in range(groups):
        here = slice(group * rows, (group + 1) * rows)
        for part in range(2):
            near = main[part, here, :length] + (left[part, here, :] + left_far[part, here, :])
            far = main[part, here, length:]
            if group * rows < length:
                near = near + above_left[part, here, :]
                far = far + above_right[part, here, :]
            outgoing[group, part, :, :length] = near
            outgoing[group, part, :, length:] = far


def combine(main, left, left_far, above_left, above_right, groups):
    tile_px = main.shape[1]
    vmem = pl.BlockSpec(memory_space=pltpu.VMEM)
    return pl.pallas_call(
        combine_kernel,
        out_shape=jax.ShapeDtypeStruct((groups, 2, tile_px // groups, tile_px), jnp.float32),
        in_specs=[vmem] * 5,
        out_specs=vmem,
        compiler_params=pltpu.CompilerParams(vmem_limit_bytes=SMALL_VMEM_BYTES),
        name="combine",
    )(main, left, left_far, above_left, above_right)


def fit_kernel(spectra, step, rate, data, fitted):
    energies, _, rows, width = data.shape
    materials = step.shape[0]
    cols = 2 * LANES
    blocks = width // cols

    def fit_block(number, carry):
        row = pl.multiple_of(number // blocks * 8, 8)
        col = pl.multiple_of(number % blocks * cols, cols)
        here = (pl.ds(row, 8), pl.ds(col, cols))
        target = [None] * materials
        for part in range(2):
            for energy in range(energies):
                value = data[(energy, part) + here]
                for m in range(materials):
                    term = spectra[part, energy * materials + m] * value
                    target[m] = term if target[m] is None else target[m] + term
        target = [rate[0] * value for value in target]
        start = tuple(jnp.maximum(value, 0.0) for value in target)

        def descend(number, coefficients):
            moved = []
            for m in range(materials):
                total = target[m]
                for n in range(materials):
                    total = total + step[m, n] * coefficients[n]
                moved.append(jnp.maximum(total, 0.0))
            return tuple(moved)

        coefficients = lax.fori_loop(1, FIT_STEPS, descend, start)
        for part in range(2):
            for energy in range(energies):
                total = spectra[part, energy * materials] * coefficients[0]
                for m in range(1, materials):
                    total = total + spectra[part, energy * materials + m] * coefficients[m]
                fitted[(energy, part) + here] = total
        return carry

    lax.fori_loop(0, rows // 8 * blocks, fit_block, 0)


def fit_spectra(data, materials):
    gram = jnp.einsum("rem,ren->mn", materials, materials, precision=lax.Precision.HIGHEST)
    rate = 1.0 / jnp.trace(gram)
    step = jnp.eye(gram.shape[0], dtype=jnp.float32) - rate * gram
    smem = pl.BlockSpec(memory_space=pltpu.SMEM)
    vmem = pl.BlockSpec(memory_space=pltpu.VMEM)
    return pl.pallas_call(
        fit_kernel,
        out_shape=jax.ShapeDtypeStruct(data.shape, jnp.float32),
        in_specs=[smem, smem, smem, vmem],
        out_specs=vmem,
        compiler_params=pltpu.CompilerParams(vmem_limit_bytes=SMALL_VMEM_BYTES),
        name="fit_spectra",
    )(materials.reshape(2, -1), step, rate.reshape(1), data)


def body(object_tiles, probe_wave, measured, positions, materials):
    own = object_tiles[0, :, 0]
    tile_px = own.shape[-1]
    length = probe_wave.shape[-1]
    tiles = lax.axis_size("tile")
    half = tiles // 2
    last = half - 1

    def move(value, pairs):
        return lax.ppermute(value, "tile", [(s % tiles, d % tiles) for s, d in pairs])

    lower_left = move(own[:, :length, :length], [(t, t - TILE_COLS) for t in range(tiles)])
    right_step = move(own[:, :, :length], [(0, last), (half, half + last)])
    corner_step = move(
        own[:, :length, :length], [(TILE_COLS, half + TILE_COLS), (half + TILE_COLS, TILE_COLS)]
    )
    lower_right = move(own[:, :length, length:], [(t, t - TILE_COLS) for t in range(tiles)])
    right_step, columns = lax.optimization_barrier((right_step, own[:, :, :length]))
    right = move(columns, [(t, t - 1) for t in range(tiles) if t % half])
    right_far = move(right_step, [(last, half + last), (half + last, last)])
    corner = move(lower_left, [(t, t - 1) for t in range(tiles) if t % half])
    corner_far = move(corner_step, [(TILE_COLS, last), (half + TILE_COLS, half + last)])

    halos = (right, right_far, lower_left, lower_right, corner, corner_far)
    main, to_right, to_lower_left, to_lower_right, to_corner = patch_gradients(
        positions[0], own, halos, probe_wave[0], measured[0, 0]
    )
    beside = move(to_corner, [(t, t + 1) for t in range(tiles)])
    left_step = move(to_right, [(last, 0), (half + last, half)])
    above_right = move(to_lower_right, [(t, t + TILE_COLS) for t in range(tiles)])
    beside, to_right = lax.optimization_barrier((beside, to_right))
    left = move(to_right, [(t, t + 1) for t in range(tiles) if t % half != last])
    above_left = move(to_lower_left + beside, [(t, t + TILE_COLS) for t in range(tiles)])
    left_far = move(left_step, [(0, half), (half, 0)])
    groups = lax.axis_size("energy")
    outgoing = combine(main, left, left_far, above_left, above_right, groups)
    arrived = lax.all_to_all(outgoing, "energy", split_axis=0, concat_axis=0, tiled=True)
    spectra = fit_spectra(arrived, materials)
    returned = lax.all_to_all(spectra, "energy", split_axis=0, concat_axis=0, tiled=True)
    return returned.transpose(1, 0, 2, 3).reshape(1, 2, 1, tile_px, tile_px)


def solution(mesh):
    in_specs = (
        P("energy", None, "tile", None, None),
        P("energy", None, None, None),
        P("energy", "tile", None, None, None),
        P("tile", None, None),
        P(),
    )
    out_specs = P("energy", None, "tile", None, None)
    return jax.shard_map(body, mesh=mesh, in_specs=in_specs, out_specs=out_specs, check_vma=False)
```

```python
import functools
import math

import jax
import jax.numpy as jnp
import ml_dtypes
import numpy as np
from jax import lax
from jax.experimental import pallas as pl
from jax.experimental.pallas import tpu as pltpu
from jax.sharding import PartitionSpec as P

TILE_COLS = 4
FIT_STEPS = 10
AMPLITUDE_FLOOR = 0.5
LANES = 128
GROUP = 8
VMEM_BYTES = 48 * 2**20


def fourier_tables(length):
    counter = np.arange(length)
    angles = 2.0 * np.pi / length * (counter[:, None] * counter[None, :] % length)
    cosine, sine = np.cos(angles), np.sin(angles)
    left_table = np.block([[cosine, sine], [-sine, cosine]])
    right_table = np.block([[cosine, -sine], [sine, cosine]])
    return [t.astype(np.float32).astype(ml_dtypes.bfloat16) for t in (left_table, right_table)]


def times(left, right):
    return jnp.dot(left, right, preferred_element_type=jnp.float32)


def transforms(stacked, left_table, right_table):
    length = stacked[0].shape[1]
    inner = [times(left_table, value).astype(jnp.bfloat16) for value in stacked]
    beside = [jnp.concatenate([value[:length], value[length:]], 1) for value in inner]
    return [times(value, right_table) for value in beside]


def stack(real_part, imag_part):
    return jnp.concatenate([real_part.astype(jnp.bfloat16), imag_part.astype(jnp.bfloat16)], 0)


def gradient_kernel(
    corners, own, right, right_far, lower_left, lower_right, corner, corner_far, probe, measured,
    left_table, right_table, main_out, right_out, lower_left_out, lower_right_out, corner_out,
    field, grad, amplitudes, arrived,
):
    count, length = measured.shape[0], measured.shape[1]
    group = math.gcd(GROUP, count)

    def fetch(first):
        some = pl.ds(first * group, group)
        return pltpu.make_async_copy(measured.at[some], amplitudes.at[some], arrived.at[first])

    for first in range(count // group):
        fetch(first).start()
    tile_px = own.shape[1]
    across, beyond = tile_px // LANES, length // LANES
    for part in range(2):
        for block in range(across):
            cols = slice(block * LANES, (block + 1) * LANES)
            field[part, block, :tile_px, :] = own[part, :, cols]
        for block in range(beyond):
            cols = slice(block * LANES, (block + 1) * LANES)
            field[part, block, tile_px:, :] = lower_left[part, :, cols]
            field[part, beyond + block, tile_px:, :] = lower_right[part, :, cols]
            field[part, across + block, :tile_px, :] = right[part, :, cols] + right_far[part, :, cols]
            field[part, across + block, tile_px:, :] = (
                corner[part, :, cols] + corner_far[part, :, cols]
            )
    grad[...] = jnp.zeros_like(grad)
    lane = lax.broadcasted_iota(jnp.int32, (length, LANES), 1)
    floor = (AMPLITUDE_FLOOR * length) ** 2

    def place(number):
        row, col = corners[number, 0], corners[number, 1]
        return pl.ds(row, length), col // LANES, col % LANES

    def exit_wave(number):
        rows, block, shift = place(number)
        head = lane < LANES - shift
        piece = []
        for part in range(2):
            turned = [
                pltpu.roll(field[part, block + i, rows, :], (LANES - shift) % LANES, 1)
                for i in range(beyond + 1)
            ]
            piece.append(
                jnp.concatenate(
                    [jnp.where(head, turned[i], turned[i + 1]) for i in range(beyond)], 1
                )
            )
        probe_real, probe_imag = probe[0], probe[1]
        return stack(
            probe_real * piece[0] - probe_imag * piece[1],
            probe_real * piece[1] + probe_imag * piece[0],
        )

    def change(number, far):
        far_real, far_imag = far[:, :length], far[:, length:]
        power = jnp.maximum(far_real * far_real + far_imag * far_imag, floor)
        factor = amplitudes[number].astype(jnp.float32) * (length * lax.rsqrt(power)) - 1.0
        return stack(factor * far_real, factor * far_imag)

    def add_terms(number, back):
        rows, block, shift = place(number)
        probe_real, probe_imag = probe[0], probe[1]
        back_real, back_imag = back[:, :length], back[:, length:]
        terms = (
            probe_real * back_real + probe_imag * back_imag,
            probe_real * back_imag - probe_imag * back_real,
        )
        tail = lane >= shift
        for part in range(2):
            turned = [
                pltpu.roll(terms[part][:, i * LANES : (i + 1) * LANES], shift, 1)
                for i in range(beyond)
            ]
            grad[part, block, rows, :] += jnp.where(tail, turned[0], 0.0)
            for i in range(1, beyond):
                grad[part, block + i, rows, :] += jnp.where(tail, turned[i], turned[i - 1])
            grad[part, block + beyond, rows, :] += jnp.where(tail, 0.0, turned[beyond - 1])

    def add_group(first, carry):
        numbers = [first * group + i for i in range(group)]
        waves = [exit_wave(number) for number in numbers]
        far = transforms(waves, left_table[...], right_table[...])
        fetch(first).wait()
        changes = [change(number, value) for number, value in zip(numbers, far)]
        back = transforms(changes, right_table[...], left_table[...])
        for number, value in zip(numbers, back):
            add_terms(number, value)
        return carry

    lax.fori_loop(0, count // group, add_group, 0)
    peak = jnp.max(probe[0] * probe[0] + probe[1] * probe[1], keepdims=True)
    scale = 1.0 / (peak * float(length * length))
    for part in range(2):
        for block in range(across):
            cols = slice(block * LANES, (block + 1) * LANES)
            main_out[part, :, cols] = own[part, :, cols] + grad[part, block, :tile_px, :] * scale
        for block in range(beyond):
            cols = slice(block * LANES, (block + 1) * LANES)
            lower_left_out[part, :, cols] = grad[part, block, tile_px:, :] * scale
            lower_right_out[part, :, cols] = grad[part, beyond + block, tile_px:, :] * scale
            right_out[part, :, cols] = grad[part, across + block, :tile_px, :] * scale
            corner_out[part, :, cols] = grad[part, across + block, tile_px:, :] * scale


def patch_gradients(corners, own, halos, probe, measured):
    count, length = measured.shape[0], measured.shape[1]
    tile_px = own.shape[1]
    left_table, right_table = (jnp.asarray(t) for t in fourier_tables(length))
    extent = tile_px + length
    vmem = pl.BlockSpec(memory_space=pltpu.VMEM)
    plane = pltpu.VMEM((2, extent // LANES, extent, LANES), jnp.float32)
    f32 = functools.partial(jax.ShapeDtypeStruct, dtype=jnp.float32)
    square = f32((2, length, length))
    return pl.pallas_call(
        gradient_kernel,
        out_shape=[
            f32((2, tile_px, tile_px)), f32((2, tile_px, length)), square, square, square,
        ],
        in_specs=[
            pl.BlockSpec(memory_space=pltpu.SMEM), *[vmem] * 8,
            pl.BlockSpec(memory_space=pl.ANY), vmem, vmem,
        ],
        out_specs=[vmem] * 5,
        scratch_shapes=[
            plane, plane, pltpu.VMEM(measured.shape, measured.dtype),
            pltpu.SemaphoreType.DMA((count // math.gcd(GROUP, count),)),
        ],
        compiler_params=pltpu.CompilerParams(vmem_limit_bytes=VMEM_BYTES),
        cost_estimate=pl.CostEstimate(
            flops=count * 32 * length**3, bytes_accessed=2**23, transcendentals=0
        ),
        name="patch_gradients",
    )(corners, own, *halos, probe, measured, left_table, right_table)


def fit_kernel(spectra, step, rate, data, fitted):
    energies, _, rows, width = data.shape
    materials = step.shape[0]
    cols = math.gcd(4 * LANES, width)
    blocks = width // cols

    def fit_block(number, carry):
        row = pl.multiple_of(number // blocks * 8, 8)
        col = pl.multiple_of(number % blocks * cols, cols)
        here = (pl.ds(row, 8), pl.ds(col, cols))
        target = [None] * materials
        for part in range(2):
            for energy in range(energies):
                value = data[(energy, part) + here]
                for m in range(materials):
                    term = spectra[part, energy * materials + m] * value
                    target[m] = term if target[m] is None else target[m] + term
        target = [rate[0] * value for value in target]
        start = tuple(jnp.maximum(value, 0.0) for value in target)

        def descend(number, coefficients):
            moved = []
            for m in range(materials):
                total = target[m]
                for n in range(materials):
                    total = total + step[m, n] * coefficients[n]
                moved.append(jnp.maximum(total, 0.0))
            return tuple(moved)

        coefficients = lax.fori_loop(1, FIT_STEPS, descend, start, unroll=True)
        for part in range(2):
            for energy in range(energies):
                total = spectra[part, energy * materials] * coefficients[0]
                for m in range(1, materials):
                    total = total + spectra[part, energy * materials + m] * coefficients[m]
                fitted[(energy, part) + here] = total
        return carry

    lax.fori_loop(0, rows // 8 * blocks, fit_block, 0)


def fit_spectra(data, materials):
    gram = jnp.einsum("rem,ren->mn", materials, materials, precision=lax.Precision.HIGHEST)
    rate = 1.0 / jnp.trace(gram)
    step = jnp.eye(gram.shape[0], dtype=jnp.float32) - rate * gram
    smem = pl.BlockSpec(memory_space=pltpu.SMEM)
    vmem = pl.BlockSpec(memory_space=pltpu.VMEM)
    return pl.pallas_call(
        fit_kernel,
        out_shape=jax.ShapeDtypeStruct(data.shape, jnp.float32),
        in_specs=[smem, smem, smem, vmem],
        out_specs=vmem,
        compiler_params=pltpu.CompilerParams(vmem_limit_bytes=VMEM_BYTES),
        name="fit_spectra",
    )(materials.reshape(2, -1), step, rate.reshape(1), data)


def body(object_tiles, probe_wave, measured, positions, materials):
    own = object_tiles[0, :, 0]
    tile_px = own.shape[-1]
    length = probe_wave.shape[-1]
    tiles = lax.axis_size("tile")
    half = tiles // 2
    last = half - 1

    def move(value, pairs):
        return lax.ppermute(value, "tile", [(s % tiles, d % tiles) for s, d in pairs])

    lower_left = move(own[:, :length, :length], [(t, t - TILE_COLS) for t in range(tiles)])
    right_step = move(own[:, :, :length], [(0, last), (half, half + last)])
    corner_step = move(
        own[:, :length, :length], [(TILE_COLS, half + TILE_COLS), (half + TILE_COLS, TILE_COLS)]
    )
    right = move(own[:, :, :length], [(t, t - 1) for t in range(tiles) if t % half])
    lower_right = move(own[:, :length, length:], [(t, t - TILE_COLS) for t in range(tiles)])
    right_far = move(right_step, [(last, half + last), (half + last, last)])
    corner_far = move(corner_step, [(TILE_COLS, last), (half + TILE_COLS, half + last)])
    corner = move(lower_left, [(t, t - 1) for t in range(tiles) if t % half])

    halos = (right, right_far, lower_left, lower_right, corner, corner_far)
    main, to_right, to_lower_left, to_lower_right, to_corner = patch_gradients(
        positions[0], own, halos, probe_wave[0], measured[0, 0]
    )
    beside = move(to_corner, [(t, t + 1) for t in range(tiles) if t % half != last])
    diagonal = move(to_corner, [(last, 2), (half + last, half + 2)])
    left_step = move(to_right, [(last, 0), (half + last, half)])
    beside, to_right, to_lower_right = lax.optimization_barrier((beside, to_right, to_lower_right))
    to_lower = jnp.concatenate([to_lower_left + beside, to_lower_right], 2)
    above = move(to_lower, [(t, t + TILE_COLS) for t in range(tiles)])
    left = move(to_right, [(t, t + 1) for t in range(tiles) if t % half != last])
    diagonal = move(diagonal, [(2, half + 2), (half + 2, 2)])
    left_far = move(left_step, [(0, half), (half, 0)])
    diagonal = move(diagonal, [(half + 2, half + TILE_COLS), (2, TILE_COLS)])
    rest = tile_px - length
    updated = (
        main
        + jnp.pad(left + left_far, ((0, 0), (0, 0), (0, rest)))
        + jnp.pad(above, ((0, 0), (0, rest), (0, 0)))
        + jnp.pad(diagonal, ((0, 0), (0, rest), (0, rest)))
    )
    groups = lax.axis_size("energy")
    outgoing = updated.reshape(2, groups, tile_px // groups, tile_px).transpose(1, 0, 2, 3)
    arrived = lax.all_to_all(outgoing, "energy", split_axis=0, concat_axis=0, tiled=True)
    spectra = fit_spectra(arrived, materials)
    returned = lax.all_to_all(spectra, "energy", split_axis=0, concat_axis=0, tiled=True)
    return returned.transpose(1, 0, 2, 3).reshape(1, 2, 1, tile_px, tile_px)


def solution(mesh):
    in_specs = (
        P("energy", None, "tile", None, None),
        P("energy", None, None, None),
        P("energy", "tile", None, None, None),
        P("tile", None, None),
        P(),
    )
    out_specs = P("energy", None, "tile", None, None)
    return jax.shard_map(body, mesh=mesh, in_specs=in_specs, out_specs=out_specs, check_vma=False)
```

```python
import functools
import math

import jax
import jax.numpy as jnp
import ml_dtypes
import numpy as np
from jax import lax
from jax.experimental import pallas as pl
from jax.experimental.pallas import tpu as pltpu
from jax.sharding import PartitionSpec as P

TILE_COLS = 4
FIT_STEPS = 10
AMPLITUDE_FLOOR = 0.5
LANES = 128
GROUP = 8
VMEM_BYTES = 48 * 2**20


def fourier_tables(length):
    counter = np.arange(length)
    angles = 2.0 * np.pi / length * (counter[:, None] * counter[None, :] % length)
    cosine, sine = np.cos(angles), np.sin(angles)
    left_table = np.block([[cosine, sine], [-sine, cosine]])
    right_table = np.block([[cosine, -sine], [sine, cosine]])
    return [t.astype(np.float32).astype(ml_dtypes.bfloat16) for t in (left_table, right_table)]


def times(left, right):
    return jnp.dot(left, right, preferred_element_type=jnp.float32)


def transforms(stacked, left_table, right_table):
    length = stacked[0].shape[1]
    inner = [times(left_table, value).astype(jnp.bfloat16) for value in stacked]
    beside = [jnp.concatenate([value[:length], value[length:]], 1) for value in inner]
    return [times(value, right_table) for value in beside]


def stack(real_part, imag_part):
    return jnp.concatenate([real_part.astype(jnp.bfloat16), imag_part.astype(jnp.bfloat16)], 0)


def gradient_kernel(
    corners, own, right, right_far, lower_left, lower_right, corner, corner_far, probe, measured,
    left_table, right_table, main_out, right_out, lower_left_out, lower_right_out, corner_out,
    field, grad, amplitudes, arrived,
):
    count, length = measured.shape[0], measured.shape[1]
    group = math.gcd(GROUP, count)

    def fetch(first):
        some = pl.ds(first * group, group)
        return pltpu.make_async_copy(measured.at[some], amplitudes.at[some], arrived.at[first])

    for first in range(count // group):
        fetch(first).start()
    tile_px = own.shape[1]
    across, beyond = tile_px // LANES, length // LANES
    for part in range(2):
        for block in range(across):
            cols = slice(block * LANES, (block + 1) * LANES)
            field[part, block, :tile_px, :] = own[part, :, cols]
        for block in range(beyond):
            cols = slice(block * LANES, (block + 1) * LANES)
            field[part, block, tile_px:, :] = lower_left[part, :, cols]
            field[part, beyond + block, tile_px:, :] = lower_right[part, :, cols]
            field[part, across + block, :tile_px, :] = right[part, :, cols] + right_far[part, :, cols]
            field[part, across + block, tile_px:, :] = (
                corner[part, :, cols] + corner_far[part, :, cols]
            )
    grad[...] = jnp.zeros_like(grad)
    lane = lax.broadcasted_iota(jnp.int32, (length, LANES), 1)
    floor = (AMPLITUDE_FLOOR * length) ** 2

    def place(number):
        row, col = corners[number, 0], corners[number, 1]
        return pl.ds(row, length), col // LANES, col % LANES

    def exit_wave(number):
        rows, block, shift = place(number)
        head = lane < LANES - shift
        piece = []
        for part in range(2):
            turned = [
                pltpu.roll(field[part, block + i, rows, :], (LANES - shift) % LANES, 1)
                for i in range(beyond + 1)
            ]
            piece.append(
                jnp.concatenate(
                    [jnp.where(head, turned[i], turned[i + 1]) for i in range(beyond)], 1
                )
            )
        probe_real, probe_imag = probe[0], probe[1]
        return stack(
            probe_real * piece[0] - probe_imag * piece[1],
            probe_real * piece[1] + probe_imag * piece[0],
        )

    def change(number, far):
        far_real, far_imag = far[:, :length], far[:, length:]
        power = jnp.maximum(far_real * far_real + far_imag * far_imag, floor)
        factor = amplitudes[number].astype(jnp.float32) * (length * lax.rsqrt(power)) - 1.0
        return stack(factor * far_real, factor * far_imag)

    def add_terms(number, back):
        rows, block, shift = place(number)
        probe_real, probe_imag = probe[0], probe[1]
        back_real, back_imag = back[:, :length], back[:, length:]
        terms = (
            probe_real * back_real + probe_imag * back_imag,
            probe_real * back_imag - probe_imag * back_real,
        )
        tail = lane >= shift
        for part in range(2):
            turned = [
                pltpu.roll(terms[part][:, i * LANES : (i + 1) * LANES], shift, 1)
                for i in range(beyond)
            ]
            grad[part, block, rows, :] += jnp.where(tail, turned[0], 0.0)
            for i in range(1, beyond):
                grad[part, block + i, rows, :] += jnp.where(tail, turned[i], turned[i - 1])
            grad[part, block + beyond, rows, :] += jnp.where(tail, 0.0, turned[beyond - 1])

    def add_group(first, carry):
        numbers = [first * group + i for i in range(group)]
        waves = [exit_wave(number) for number in numbers]
        far = transforms(waves, left_table[...], right_table[...])
        fetch(first).wait()
        changes = [change(number, value) for number, value in zip(numbers, far)]
        back = transforms(changes, right_table[...], left_table[...])
        for number, value in zip(numbers, back):
            add_terms(number, value)
        return carry

    lax.fori_loop(0, count // group, add_group, 0)
    peak = jnp.max(probe[0] * probe[0] + probe[1] * probe[1], keepdims=True)
    scale = 1.0 / (peak * float(length * length))
    for part in range(2):
        for block in range(across):
            cols = slice(block * LANES, (block + 1) * LANES)
            main_out[part, :, cols] = own[part, :, cols] + grad[part, block, :tile_px, :] * scale
        for block in range(beyond):
            cols = slice(block * LANES, (block + 1) * LANES)
            lower_left_out[part, :, cols] = grad[part, block, tile_px:, :] * scale
            lower_right_out[part, :, cols] = grad[part, beyond + block, tile_px:, :] * scale
            right_out[part, :, cols] = grad[part, across + block, :tile_px, :] * scale
            corner_out[part, :, cols] = grad[part, across + block, tile_px:, :] * scale


def patch_gradients(corners, own, halos, probe, measured):
    count, length = measured.shape[0], measured.shape[1]
    tile_px = own.shape[1]
    left_table, right_table = (jnp.asarray(t) for t in fourier_tables(length))
    extent = tile_px + length
    vmem = pl.BlockSpec(memory_space=pltpu.VMEM)
    plane = pltpu.VMEM((2, extent // LANES, extent, LANES), jnp.float32)
    f32 = functools.partial(jax.ShapeDtypeStruct, dtype=jnp.float32)
    square = f32((2, length, length))
    return pl.pallas_call(
        gradient_kernel,
        out_shape=[
            f32((2, tile_px, tile_px)), f32((2, tile_px, length)), square, square, square,
        ],
        in_specs=[
            pl.BlockSpec(memory_space=pltpu.SMEM), *[vmem] * 8,
            pl.BlockSpec(memory_space=pl.ANY), vmem, vmem,
        ],
        out_specs=[vmem] * 5,
        scratch_shapes=[
            plane, plane, pltpu.VMEM(measured.shape, measured.dtype),
            pltpu.SemaphoreType.DMA((count // math.gcd(GROUP, count),)),
        ],
        compiler_params=pltpu.CompilerParams(vmem_limit_bytes=VMEM_BYTES),
        cost_estimate=pl.CostEstimate(
            flops=count * 32 * length**3, bytes_accessed=2**23, transcendentals=0
        ),
        name="patch_gradients",
    )(corners, own, *halos, probe, measured, left_table, right_table)


def fit_kernel(spectra, step, rate, data, fitted):
    energies, _, rows, width = data.shape
    materials = step.shape[0]
    cols = math.gcd(4 * LANES, width)
    blocks = width // cols

    def fit_block(number, carry):
        row = pl.multiple_of(number // blocks * 8, 8)
        col = pl.multiple_of(number % blocks * cols, cols)
        here = (pl.ds(row, 8), pl.ds(col, cols))
        target = [None] * materials
        for part in range(2):
            for energy in range(energies):
                value = data[(energy, part) + here]
                for m in range(materials):
                    term = spectra[part, energy * materials + m] * value
                    target[m] = term if target[m] is None else target[m] + term
        target = [rate[0] * value for value in target]
        start = tuple(jnp.maximum(value, 0.0) for value in target)

        def descend(number, coefficients):
            moved = []
            for m in range(materials):
                total = target[m]
                for n in range(materials):
                    total = total + step[m, n] * coefficients[n]
                moved.append(jnp.maximum(total, 0.0))
            return tuple(moved)

        coefficients = lax.fori_loop(1, FIT_STEPS, descend, start, unroll=True)
        for part in range(2):
            for energy in range(energies):
                total = spectra[part, energy * materials] * coefficients[0]
                for m in range(1, materials):
                    total = total + spectra[part, energy * materials + m] * coefficients[m]
                fitted[(energy, part) + here] = total
        return carry

    lax.fori_loop(0, rows // 8 * blocks, fit_block, 0)


def fit_spectra(data, materials):
    gram = jnp.einsum("rem,ren->mn", materials, materials, precision=lax.Precision.HIGHEST)
    rate = 1.0 / jnp.trace(gram)
    step = jnp.eye(gram.shape[0], dtype=jnp.float32) - rate * gram
    smem = pl.BlockSpec(memory_space=pltpu.SMEM)
    vmem = pl.BlockSpec(memory_space=pltpu.VMEM)
    return pl.pallas_call(
        fit_kernel,
        out_shape=jax.ShapeDtypeStruct(data.shape, jnp.float32),
        in_specs=[smem, smem, smem, vmem],
        out_specs=vmem,
        compiler_params=pltpu.CompilerParams(vmem_limit_bytes=VMEM_BYTES),
        name="fit_spectra",
    )(materials.reshape(2, -1), step, rate.reshape(1), data)


def body(object_tiles, probe_wave, measured, positions, materials):
    own = object_tiles[0, :, 0]
    tile_px = own.shape[-1]
    length = probe_wave.shape[-1]
    tiles = lax.axis_size("tile")
    half = tiles // 2
    last = half - 1

    def move(value, pairs):
        return lax.ppermute(value, "tile", [(s % tiles, d % tiles) for s, d in pairs])

    lower_left = move(own[:, :length, :length], [(t, t - TILE_COLS) for t in range(tiles)])
    right_step = move(own[:, :, :length], [(0, last), (half, half + last)])
    corner_step = move(
        own[:, :length, :length], [(TILE_COLS, half + TILE_COLS), (half + TILE_COLS, TILE_COLS)]
    )
    right = move(own[:, :, :length], [(t, t - 1) for t in range(tiles) if t % half])
    lower_right = move(own[:, :length, length:], [(t, t - TILE_COLS) for t in range(tiles)])
    right_far = move(right_step, [(last, half + last), (half + last, last)])
    corner_far = move(corner_step, [(TILE_COLS, last), (half + TILE_COLS, half + last)])
    corner = move(lower_left, [(t, t - 1) for t in range(tiles) if t % half])

    halos = (right, right_far, lower_left, lower_right, corner, corner_far)
    main, to_right, to_lower_left, to_lower_right, to_corner = patch_gradients(
        positions[0], own, halos, probe_wave[0], measured[0, 0]
    )
    beside = move(to_corner, [(t, t + 1) for t in range(tiles)])
    above_right = move(to_lower_right, [(t, t + TILE_COLS) for t in range(tiles)])
    left_step = move(to_right, [(last, 0), (half + last, half)])
    left = move(to_right, [(t, t + 1) for t in range(tiles) if t % half != last])
    left_far = move(left_step, [(0, half), (half, 0)])
    above_left = move(to_lower_left + beside, [(t, t + TILE_COLS) for t in range(tiles)])
    above = jnp.concatenate([above_left, above_right], 2)
    updated = (
        main
        + jnp.pad(left + left_far, ((0, 0), (0, 0), (0, tile_px - length)))
        + jnp.pad(above, ((0, 0), (0, tile_px - length), (0, 0)))
    )
    groups = lax.axis_size("energy")
    outgoing = updated.reshape(2, groups, tile_px // groups, tile_px).transpose(1, 0, 2, 3)
    arrived = lax.all_to_all(outgoing, "energy", split_axis=0, concat_axis=0, tiled=True)
    spectra = fit_spectra(arrived, materials)
    returned = lax.all_to_all(spectra, "energy", split_axis=0, concat_axis=0, tiled=True)
    return returned.transpose(1, 0, 2, 3).reshape(1, 2, 1, tile_px, tile_px)


def solution(mesh):
    in_specs = (
        P("energy", None, "tile", None, None),
        P("energy", None, None, None),
        P("energy", "tile", None, None, None),
        P("tile", None, None),
        P(),
    )
    out_specs = P("energy", None, "tile", None, None)
    return jax.shard_map(body, mesh=mesh, in_specs=in_specs, out_specs=out_specs, check_vma=False)
```

```python
import functools
import math

import jax
import jax.numpy as jnp
import ml_dtypes
import numpy as np
from jax import lax
from jax.experimental import pallas as pl
from jax.experimental.pallas import tpu as pltpu
from jax.sharding import PartitionSpec as P

TILE_COLS = 4
FIT_STEPS = 10
AMPLITUDE_FLOOR = 0.5
LANES = 128
GROUP = 8
VMEM_BYTES = 48 * 2**20


def fourier_tables(length):
    counter = np.arange(length)
    angles = 2.0 * np.pi / length * (counter[:, None] * counter[None, :] % length)
    cosine, sine = np.cos(angles), np.sin(angles)
    left_table = np.block([[cosine, sine], [-sine, cosine]])
    right_table = np.block([[cosine, -sine], [sine, cosine]])
    return [t.astype(np.float32).astype(ml_dtypes.bfloat16) for t in (left_table, right_table)]


def times(left, right):
    return jnp.dot(left, right, preferred_element_type=jnp.float32)


def transforms(stacked, left_table, right_table):
    length = stacked[0].shape[1]
    inner = [times(left_table, value).astype(jnp.bfloat16) for value in stacked]
    beside = [jnp.concatenate([value[:length], value[length:]], 1) for value in inner]
    return [times(value, right_table) for value in beside]


def stack(real_part, imag_part):
    return jnp.concatenate([real_part.astype(jnp.bfloat16), imag_part.astype(jnp.bfloat16)], 0)


def gradient_kernel(
    corners, own, right, right_far, lower_left, lower_right, corner, corner_far, probe, measured,
    left_table, right_table, main_out, right_out, lower_left_out, lower_right_out, corner_out,
    field, grad, amplitudes, arrived,
):
    count, length = measured.shape[0], measured.shape[1]
    group = math.gcd(GROUP, count)

    def fetch(first):
        some = pl.ds(first * group, group)
        return pltpu.make_async_copy(measured.at[some], amplitudes.at[some], arrived.at[first])

    for first in range(count // group):
        fetch(first).start()
    tile_px = own.shape[1]
    across, beyond = tile_px // LANES, length // LANES
    for part in range(2):
        for block in range(across):
            cols = slice(block * LANES, (block + 1) * LANES)
            field[part, block, :tile_px, :] = own[part, :, cols]
        for block in range(beyond):
            cols = slice(block * LANES, (block + 1) * LANES)
            field[part, block, tile_px:, :] = lower_left[part, :, cols]
            field[part, beyond + block, tile_px:, :] = lower_right[part, :, cols]
            field[part, across + block, :tile_px, :] = right[part, :, cols] + right_far[part, :, cols]
            field[part, across + block, tile_px:, :] = (
                corner[part, :, cols] + corner_far[part, :, cols]
            )
    grad[...] = jnp.zeros_like(grad)
    lane = lax.broadcasted_iota(jnp.int32, (length, LANES), 1)
    floor = (AMPLITUDE_FLOOR * length) ** 2

    def place(number):
        row, col = corners[number, 0], corners[number, 1]
        return pl.ds(row, length), col // LANES, col % LANES

    def exit_wave(number):
        rows, block, shift = place(number)
        head = lane < LANES - shift
        piece = []
        for part in range(2):
            turned = [
                pltpu.roll(field[part, block + i, rows, :], (LANES - shift) % LANES, 1)
                for i in range(beyond + 1)
            ]
            piece.append(
                jnp.concatenate(
                    [jnp.where(head, turned[i], turned[i + 1]) for i in range(beyond)], 1
                )
            )
        probe_real, probe_imag = probe[0], probe[1]
        return stack(
            probe_real * piece[0] - probe_imag * piece[1],
            probe_real * piece[1] + probe_imag * piece[0],
        )

    def change(number, far):
        far_real, far_imag = far[:, :length], far[:, length:]
        power = jnp.maximum(far_real * far_real + far_imag * far_imag, floor)
        factor = amplitudes[number].astype(jnp.float32) * (length * lax.rsqrt(power)) - 1.0
        return stack(factor * far_real, factor * far_imag)

    def add_terms(number, back):
        rows, block, shift = place(number)
        probe_real, probe_imag = probe[0], probe[1]
        back_real, back_imag = back[:, :length], back[:, length:]
        terms = (
            probe_real * back_real + probe_imag * back_imag,
            probe_real * back_imag - probe_imag * back_real,
        )
        tail = lane >= shift
        for part in range(2):
            turned = [
                pltpu.roll(terms[part][:, i * LANES : (i + 1) * LANES], shift, 1)
                for i in range(beyond)
            ]
            grad[part, block, rows, :] += jnp.where(tail, turned[0], 0.0)
            for i in range(1, beyond):
                grad[part, block + i, rows, :] += jnp.where(tail, turned[i], turned[i - 1])
            grad[part, block + beyond, rows, :] += jnp.where(tail, 0.0, turned[beyond - 1])

    def add_group(first, carry):
        numbers = [first * group + i for i in range(group)]
        waves = [exit_wave(number) for number in numbers]
        far = transforms(waves, left_table[...], right_table[...])
        fetch(first).wait()
        changes = [change(number, value) for number, value in zip(numbers, far)]
        back = transforms(changes, right_table[...], left_table[...])
        for number, value in zip(numbers, back):
            add_terms(number, value)
        return carry

    lax.fori_loop(0, count // group, add_group, 0)
    peak = jnp.max(probe[0] * probe[0] + probe[1] * probe[1], keepdims=True)
    scale = 1.0 / (peak * float(length * length))
    for part in range(2):
        for block in range(across):
            cols = slice(block * LANES, (block + 1) * LANES)
            main_out[part, :, cols] = own[part, :, cols] + grad[part, block, :tile_px, :] * scale
        for block in range(beyond):
            cols = slice(block * LANES, (block + 1) * LANES)
            lower_left_out[part, :, cols] = grad[part, block, tile_px:, :] * scale
            lower_right_out[part, :, cols] = grad[part, beyond + block, tile_px:, :] * scale
            right_out[part, :, cols] = grad[part, across + block, :tile_px, :] * scale
            corner_out[part, :, cols] = grad[part, across + block, tile_px:, :] * scale


def patch_gradients(corners, own, halos, probe, measured):
    count, length = measured.shape[0], measured.shape[1]
    tile_px = own.shape[1]
    left_table, right_table = (jnp.asarray(t) for t in fourier_tables(length))
    extent = tile_px + length
    vmem = pl.BlockSpec(memory_space=pltpu.VMEM)
    plane = pltpu.VMEM((2, extent // LANES, extent, LANES), jnp.float32)
    f32 = functools.partial(jax.ShapeDtypeStruct, dtype=jnp.float32)
    square = f32((2, length, length))
    return pl.pallas_call(
        gradient_kernel,
        out_shape=[
            f32((2, tile_px, tile_px)), f32((2, tile_px, length)), square, square, square,
        ],
        in_specs=[
            pl.BlockSpec(memory_space=pltpu.SMEM), *[vmem] * 8,
            pl.BlockSpec(memory_space=pl.ANY), vmem, vmem,
        ],
        out_specs=[vmem] * 5,
        scratch_shapes=[
            plane, plane, pltpu.VMEM(measured.shape, measured.dtype),
            pltpu.SemaphoreType.DMA((count // math.gcd(GROUP, count),)),
        ],
        compiler_params=pltpu.CompilerParams(vmem_limit_bytes=VMEM_BYTES),
        cost_estimate=pl.CostEstimate(
            flops=count * 32 * length**3, bytes_accessed=2**23, transcendentals=0
        ),
        name="patch_gradients",
    )(corners, own, *halos, probe, measured, left_table, right_table)


def fit_kernel(spectra, step, rate, data, fitted):
    energies, _, rows, width = data.shape
    materials = step.shape[0]
    cols = math.gcd(4 * LANES, width)
    blocks = width // cols

    def fit_block(number, carry):
        row = pl.multiple_of(number // blocks * 8, 8)
        col = pl.multiple_of(number % blocks * cols, cols)
        here = (pl.ds(row, 8), pl.ds(col, cols))
        target = [None] * materials
        for part in range(2):
            for energy in range(energies):
                value = data[(energy, part) + here]
                for m in range(materials):
                    term = spectra[part, energy * materials + m] * value
                    target[m] = term if target[m] is None else target[m] + term
        target = [rate[0] * value for value in target]
        start = tuple(jnp.maximum(value, 0.0) for value in target)

        def descend(number, coefficients):
            moved = []
            for m in range(materials):
                total = target[m]
                for n in range(materials):
                    total = total + step[m, n] * coefficients[n]
                moved.append(jnp.maximum(total, 0.0))
            return tuple(moved)

        coefficients = lax.fori_loop(1, FIT_STEPS, descend, start, unroll=True)
        for part in range(2):
            for energy in range(energies):
                total = spectra[part, energy * materials] * coefficients[0]
                for m in range(1, materials):
                    total = total + spectra[part, energy * materials + m] * coefficients[m]
                fitted[(energy, part) + here] = total
        return carry

    lax.fori_loop(0, rows // 8 * blocks, fit_block, 0)


def fit_spectra(data, materials):
    gram = jnp.einsum("rem,ren->mn", materials, materials, precision=lax.Precision.HIGHEST)
    rate = 1.0 / jnp.trace(gram)
    step = jnp.eye(gram.shape[0], dtype=jnp.float32) - rate * gram
    smem = pl.BlockSpec(memory_space=pltpu.SMEM)
    vmem = pl.BlockSpec(memory_space=pltpu.VMEM)
    return pl.pallas_call(
        fit_kernel,
        out_shape=jax.ShapeDtypeStruct(data.shape, jnp.float32),
        in_specs=[smem, smem, smem, vmem],
        out_specs=vmem,
        compiler_params=pltpu.CompilerParams(vmem_limit_bytes=VMEM_BYTES),
        name="fit_spectra",
    )(materials.reshape(2, -1), step, rate.reshape(1), data)


def body(object_tiles, probe_wave, measured, positions, materials):
    own = object_tiles[0, :, 0]
    tile_px = own.shape[-1]
    length = probe_wave.shape[-1]
    tiles = lax.axis_size("tile")
    half = tiles // 2
    last = half - 1

    def move(value, pairs):
        return lax.ppermute(value, "tile", [(s % tiles, d % tiles) for s, d in pairs])

    lower_left = move(own[:, :length, :length], [(t, t - TILE_COLS) for t in range(tiles)])
    right_step = move(own[:, :, :length], [(0, last), (half, half + last)])
    corner_step = move(
        own[:, :length, :length], [(TILE_COLS, half + TILE_COLS), (half + TILE_COLS, TILE_COLS)]
    )
    right = move(own[:, :, :length], [(t, t - 1) for t in range(tiles) if t % half])
    lower_right = move(own[:, :length, length:], [(t, t - TILE_COLS) for t in range(tiles)])
    right_far = move(right_step, [(last, half + last), (half + last, last)])
    corner_far = move(corner_step, [(TILE_COLS, last), (half + TILE_COLS, half + last)])
    corner = move(lower_left, [(t, t - 1) for t in range(tiles) if t % half])

    halos = (right, right_far, lower_left, lower_right, corner, corner_far)
    main, to_right, to_lower_left, to_lower_right, to_corner = patch_gradients(
        positions[0], own, halos, probe_wave[0], measured[0, 0]
    )
    beside = move(to_corner, [(t, t + 1) for t in range(tiles)])
    above_right = move(to_lower_right, [(t, t + TILE_COLS) for t in range(tiles)])
    left_step = move(to_right, [(last, 0), (half + last, half)])
    left = move(to_right, [(t, t + 1) for t in range(tiles) if t % half != last])
    left_step, beside = lax.optimization_barrier((left_step, beside))
    left_far = move(left_step, [(0, half), (half, 0)])
    above_left = move(to_lower_left + beside, [(t, t + TILE_COLS) for t in range(tiles)])
    above = jnp.concatenate([above_left, above_right], 2)
    updated = (
        main
        + jnp.pad(left + left_far, ((0, 0), (0, 0), (0, tile_px - length)))
        + jnp.pad(above, ((0, 0), (0, tile_px - length), (0, 0)))
    )
    groups = lax.axis_size("energy")
    outgoing = updated.reshape(2, groups, tile_px // groups, tile_px).transpose(1, 0, 2, 3)
    arrived = lax.all_to_all(outgoing, "energy", split_axis=0, concat_axis=0, tiled=True)
    spectra = fit_spectra(arrived, materials)
    returned = lax.all_to_all(spectra, "energy", split_axis=0, concat_axis=0, tiled=True)
    return returned.transpose(1, 0, 2, 3).reshape(1, 2, 1, tile_px, tile_px)


def solution(mesh):
    in_specs = (
        P("energy", None, "tile", None, None),
        P("energy", None, None, None),
        P("energy", "tile", None, None, None),
        P("tile", None, None),
        P(),
    )
    out_specs = P("energy", None, "tile", None, None)
    return jax.shard_map(body, mesh=mesh, in_specs=in_specs, out_specs=out_specs, check_vma=False)
```
